32 devices in a mesh: dp: 32 (over z, y, x, core), cent: 1.
Axes of the slice: x: 2, y: 2, z: 4, core: 2. Of those that a mesh axis runs over, the one named last changes fastest.
Arguments:
- hidden: bfloat16 [5632, 11008], P('dp', 'cent'), may hold values from -6 to 6
- residual: bfloat16 [5632, 4096], P('dp', 'cent'), may hold values from -6 to 6
- down_weight: bfloat16 [11008, 4096], P('cent', 'dp'), may hold values from -0.0546875 to 0.0546875
- gain: float32 [4096], P('cent'), may hold values from 0.1 to 1.9
- proj_weight: bfloat16 [4096, 1024], P('cent'), may hold values from -0.09375 to 0.09375
- centroids: bfloat16 [16384, 1024], P(('dp', 'cent')), may hold values from -24 to 24
Outputs:
- weighted: float32 [16384, 1024], P(('dp', 'cent'))
- counts: float32 [16384], P(('dp', 'cent'))
The draws below stay inside these ranges and needn't reach their ends.
All inputs are finite; a program needn't handle non-finite values.
Results may differ from the reference program's by a relative error of at most 0.011.
Values may be sent and summed in bfloat16 or wider, within the bound.
No kernel may reach another device: no remote copies, remote signals or barrier semaphores. Data moves between devices by JAX's collectives and lax.ppermute only.
A program may use at most 192 MiB of HBM per device.

```python
import math
import jax
import jax.numpy as jnp
from jax import lax

D = 4096
FF = 11008
E = 1024
CENT_DEV = 512
PASSAGES = 5632
CENTROIDS = 16384


def draw_centroids(key, part):
    key_base = jax.random.fold_in(key, 0)
    normal_base = jax.random.normal(key_base, (CENTROIDS, E), jnp.float32)
    row_scale = jnp.full((CENTROIDS, 1), 0.15, jnp.float32)
    return jnp.clip(normal_base * row_scale, -24.0, 24.0).astype(jnp.bfloat16)


def block_scale(rng, dims, cuts, least, high):
    factor_of = 1.0
    for dim, blocks in cuts:
        steps = jax.random.uniform(jax.random.fold_in(jax.random.fold_in(rng, 6), dim), (blocks,), jnp.float32, least / len(cuts), high / len(cuts))
        factor_of = factor_of * jnp.repeat(jnp.exp(steps), dims[dim] // blocks).reshape((-1,) + (1,) * (len(dims) - 1 - dim))
    return factor_of


def scatter_about(key, shape, spread, bound, cuts=(), kind=jnp.bfloat16):
    factor_of = block_scale(key, shape, cuts, -0.22, 0.18) if cuts else 1.0
    values = jax.random.normal(key, shape, jnp.float32) * spread * factor_of
    return jnp.minimum(jnp.maximum(values, -bound), bound).astype(kind)


def setup_inputs(seed: int = 0) -> dict:
    seeds = jax.random.split(jax.random.key(seed), 7)
    return {
        "hidden": scatter_about(seeds[0], (PASSAGES, FF), 1.0, 6.0, ((0, 32),)),
        "residual": scatter_about(seeds[1], (PASSAGES, D), 1.0, 6.0, ((0, 32),)),
        "down_weight": scatter_about(seeds[2], (FF, D), FF ** -0.5, 0.0546875, ((1, 32),)),
        "gain": jnp.clip(1.0 + 0.18 * jax.random.normal(seeds[3], (D,), jnp.float32), 0.1, 1.9),
        "proj_weight": scatter_about(seeds[4], (D, E), D ** -0.5, 0.09375),
        "centroids": draw_centroids(jax.random.fold_in(seeds[6], 71), 0),
    }


def reference(hidden, residual, down_weight, gain, proj_weight, centroids):
    layer_out = jnp.dot(hidden, down_weight, preferred_element_type=jnp.float32) + residual.astype(jnp.float32)
    normed = (layer_out * gain).astype(jnp.bfloat16)
    raw_embed = jnp.dot(normed, proj_weight, preferred_element_type=jnp.float32)
    embed = (raw_embed * lax.rsqrt(lax.optimization_barrier(jnp.mean(raw_embed * raw_embed, axis=1, keepdims=True)) + 1e-06)).astype(jnp.bfloat16)
    inverse = 1.0 / (math.sqrt(E) * 0.05)
    blocks = centroids.reshape(CENTROIDS // CENT_DEV, CENT_DEV, E)

    def max_pass(carry, block_rows):
        run_max, run_total = carry
        scores = jnp.dot(embed, block_rows.T, preferred_element_type=jnp.float32) * inverse
        new_max = jnp.maximum(run_max, lax.optimization_barrier(jnp.max(scores, axis=1)))
        new_total = run_total * jnp.exp(run_max - new_max) + lax.optimization_barrier(jnp.sum(jnp.exp(scores - new_max[:, None]), axis=1))
        return ((new_max, new_total), None)
    start = (jnp.full((PASSAGES,), -jnp.inf, jnp.float32), jnp.zeros((PASSAGES,), jnp.float32))
    (row_max, row_total), _ = lax.scan(max_pass, start, blocks)
    log_total = row_max + jnp.log(row_total)
    scale_up = CENTROIDS / PASSAGES

    def sum_pass(block_rows):
        scores = jnp.dot(embed, block_rows.T, preferred_element_type=jnp.float32) * inverse
        probability = jnp.exp(scores - log_total[:, None])
        block_counts = scale_up * lax.optimization_barrier(jnp.sum(probability, axis=0))
        prob_low = probability.astype(jnp.bfloat16)
        block_sums = scale_up * jnp.dot(prob_low.T, embed, preferred_element_type=jnp.float32)
        return (block_sums, block_counts)
    weighted, counts = lax.map(sum_pass, blocks)
    return (weighted.reshape(CENTROIDS, E), counts.reshape(CENTROIDS))
```

```python
import math

import jax
import jax.numpy as jnp
from jax import lax
from jax.sharding import PartitionSpec as P


F32 = jnp.float32
BF16 = jnp.bfloat16


def dot(a, b):
    return jnp.dot(a, b, preferred_element_type=F32)


def make_body(n, plane, lines):
    line_bits = lines.bit_length() - 1

    def hop(v, k):
        return lax.ppermute(v, "dp", [(i, i ^ k) for i in range(n)])

    planes = [[z * plane + q for q in range(plane)] for z in range(lines)]

    def flips(v, bits):
        for a, bit in enumerate(bits):
            v = jnp.where(bit == 1, jnp.flip(v, a), v)
        return v

    def gather_plane(slot):
        half = slot.shape[0] // 2
        a, b = slot[:half], slot[half:]
        a = jnp.concatenate([a, hop(a, 2)])
        b = jnp.concatenate([b, hop(b, 4)])
        ay, bx = hop(a, 4), hop(b, 2)
        return jnp.concatenate([a, ay, b, bx])

    def plane_order(v, half):
        v = v.reshape(2, 2, 2, half)
        a, b = v[0], v[1]
        return jnp.concatenate([a, jnp.swapaxes(b, 0, 1)], axis=2)

    def plane_order_back(v, half):
        a, b = v[..., :half], v[..., half:]
        return jnp.stack([a, jnp.swapaxes(b, 0, 1)]).reshape(-1)

    def lse(parts):
        v = jnp.stack(parts)
        top = jnp.max(v, axis=0)
        return top + jnp.log(jnp.sum(jnp.exp(v - top), axis=0))

    def body(hidden, residual, down_weight, gain, proj_weight, centroids):
        me = lax.axis_index("dp")
        bits = [(me >> k) & 1 for k in range(n.bit_length() - 1)]
        z_bits = bits[::-1][:line_bits]
        rows, hid = hidden.shape
        share = hid // n
        feat = residual.shape[1]
        width = proj_weight.shape[1]

        z_dims = (2,) * line_bits
        blocks = hidden.reshape(rows, lines, plane, share).transpose(1, 2, 0, 3)
        blocks = flips(blocks.reshape(*z_dims, plane, rows, share), z_bits)
        blocks = blocks.reshape(lines, plane, rows, share).transpose(1, 0, 2, 3)
        blocks = lax.all_to_all(blocks, "dp", 0, 0, tiled=True, axis_index_groups=planes)

        down_rows = lax.all_to_all(down_weight, "dp", 0, 1, tiled=True)
        own = gain[:, None] * proj_weight.astype(F32)
        own_hi = own.astype(BF16)
        full = lax.all_gather(own, "cent", axis=0, tiled=True)
        full_hi = full.astype(BF16)
        full_lo = (full - full_hi.astype(F32)).astype(BF16)
        fold = (dot(down_rows, full_hi) + dot(down_rows, full_lo)).astype(BF16)
        direct = dot(residual, own_hi)

        pair = jnp.concatenate([centroids, hop(centroids, 1)])

        part = 0.0
        for k in range(lines):
            block = fold if k == 0 else hop(fold, k * plane)
            part = part + dot(blocks[:, k].reshape(plane * rows, share), block)
        part = part.astype(BF16).reshape(plane, rows, width)
        part = lax.all_to_all(part, "dp", 0, 0, tiled=True, axis_index_groups=planes)
        raw = jnp.sum(part.astype(F32), axis=0) + direct
        raw = lax.psum(raw, "cent")
        embed = (raw * lax.rsqrt(jnp.mean(raw * raw, axis=1, keepdims=True) + 1e-06)).astype(BF16)

        inverse = 1.0 / (math.sqrt(width) * 0.05)
        half = rows // 2
        slots = [gather_plane(embed if k == 0 else hop(embed, k * plane)) for k in range(lines)]
        scores, local = [], []
        for block in slots:
            s = lax.dot_general(block, pair, (((1,), (1,)), ((), ())), preferred_element_type=F32)
            s = s * inverse
            top = jnp.max(s, axis=1)
            scores.append(s)
            local.append(top + jnp.log(jnp.sum(jnp.exp(s - top[:, None]), axis=1)))

        v = jnp.stack([plane_order(x, half) for x in local])
        v = flips(v.reshape(*z_dims, 2, 2, rows), z_bits + [bits[2], bits[1]])
        v = lse([v] + [hop(v, k) for k in range(2, plane, 2)])
        v = lse([v] + [hop(v, k * plane) for k in range(1, lines)])
        if lax.axis_size("cent") > 1:
            top = lax.pmax(v, "cent")
            v = top + jnp.log(lax.psum(jnp.exp(v - top), "cent"))
        v = flips(v, z_bits + [bits[2], bits[1]]).reshape(lines, 2, 2, rows)

        counts, weighted = 0.0, 0.0
        for k in range(lines):
            total = plane_order_back(v[k], half)
            prob = jnp.exp(scores[k] - total[:, None])
            counts = counts + jnp.sum(prob, axis=0)
            weighted = weighted + lax.dot_general(
                prob.astype(BF16), slots[k], (((0,), (0,)), ((), ())), preferred_element_type=F32
            )
        cents = centroids.shape[0]
        scale_up = cents * n * lax.axis_size("cent") / (rows * n)
        far = hop(weighted[cents:].astype(BF16), 1)
        far_counts = hop(counts[cents:], 1)
        weighted = scale_up * (weighted[:cents] + far.astype(F32))
        counts = scale_up * (counts[:cents] + far_counts)
        return weighted, counts

    return body


def solution(mesh):
    n = mesh.shape["dp"]
    plane = 8
    lines = n // plane
    in_specs = (
        P("dp", "cent"),
        P("dp", "cent"),
        P("cent", "dp"),
        P("cent"),
        P("cent", None),
        P(("dp", "cent"), None),
    )
    out_specs = (P(("dp", "cent"), None), P(("dp", "cent")))
    return jax.shard_map(
        make_body(n, plane, lines), mesh=mesh, in_specs=in_specs, out_specs=out_specs, check_vma=False
    )
```

```python
import math

import jax
import jax.numpy as jnp
from jax import lax
from jax.experimental import pallas as pl
from jax.experimental.pallas import tpu as pltpu
from jax.sharding import PartitionSpec as P


F32 = jnp.float32
BF16 = jnp.bfloat16
PLANE = 8
QUAD = 4


def dot(a, b):
    return jnp.dot(a, b, preferred_element_type=F32)


def after(v, *others):
    return lax.optimization_barrier((v, *others))[0]


def lse(parts):
    top = parts[0]
    for p in parts[1:]:
        top = jnp.maximum(top, p)
    return top + jnp.log(sum(jnp.exp(p - top) for p in parts))


def weigh_kernel(count, *refs):
    scores, totals, blocks = refs[:count], refs[count : 2 * count], refs[2 * count : 3 * count]
    weighted, counts = refs[3 * count :]
    sums, masses = 0.0, 0.0
    for s, t, b in zip(scores, totals, blocks):
        prob = jnp.exp(s[...] - t[...])
        masses = masses + jnp.sum(prob, axis=1, keepdims=True)
        sums = sums + dot(prob.astype(BF16), b[...])
    weighted[...] = sums.astype(weighted.dtype)
    counts[...] = masses


def weigh(scores, totals, blocks, start, size, dtype, scale):
    count = len(scores)
    width = blocks[0].shape[1]
    tile = math.gcd(size, 256)
    first = start // tile
    passages = count * blocks[0].shape[0]
    whole = lambda a: pl.BlockSpec(a.shape, lambda i: (0, 0))
    return pl.pallas_call(
        lambda *refs: weigh_kernel(count, *refs),
        grid=(size // tile,),
        in_specs=[pl.BlockSpec((tile, s.shape[1]), lambda i: (first + i, 0)) for s in scores]
        + [whole(t) for t in totals]
        + [whole(b) for b in blocks],
        out_specs=[pl.BlockSpec((tile, width), lambda i: (i, 0)), pl.BlockSpec((tile, 1), lambda i: (i, 0))],
        out_shape=[jax.ShapeDtypeStruct((size, width), dtype), jax.ShapeDtypeStruct((size, 1), F32)],
        compiler_params=pltpu.CompilerParams(vmem_limit_bytes=48 * 2**20),
        cost_estimate=pl.CostEstimate(
            flops=2 * passages * size * width,
            bytes_accessed=passages * (4 * size + 2 * width) + 4 * size * width,
            transcendentals=passages * size,
        ),
    )(*scores, *totals, *blocks)


def deal_kernel(position, hidden, blocks):
    share = blocks.shape[2]
    for d in range(blocks.shape[0]):
        blocks[position[d]] = hidden[:, d * share : (d + 1) * share]


def deal(hidden, position):
    rows, hid = hidden.shape
    n = position.shape[0]
    vmem = pl.BlockSpec(memory_space=pltpu.VMEM)
    return pl.pallas_call(
        deal_kernel,
        in_specs=[pl.BlockSpec(memory_space=pltpu.SMEM), vmem],
        out_specs=vmem,
        out_shape=jax.ShapeDtypeStruct((n, rows, hid // n), hidden.dtype),
        compiler_params=pltpu.CompilerParams(vmem_limit_bytes=32 * 2**20),
        cost_estimate=pl.CostEstimate(flops=0, bytes_accessed=4 * rows * hid, transcendentals=0),
    )(position, hidden)


def arrivals(lines):
    table = []
    for z in range(lines):
        near = [(s, w, z - s if w == 0 else z + s) for s in range(1, lines) for w in (1, 0)]
        table.append([e for e in near if 0 <= e[2] < lines])
    return table


def make_body(n, lines):
    table = arrivals(lines)

    def hop(v, k):
        return lax.ppermute(v, "dp", [(i, i ^ k) for i in range(n)])

    def up(v):
        return lax.ppermute(v, "dp", [(i, i + PLANE) for i in range(n - PLANE)])

    def down(v):
        return lax.ppermute(v, "dp", [(i + PLANE, i) for i in range(n - PLANE)])

    def choose(line, values):
        out = values[-1]
        for z in range(lines - 2, -1, -1):
            if values[z] is not out:
                out = jnp.where(line <= z, values[z], out)
        return out

    def gather(v):
        first = [v]
        for k in range(1, lines):
            first.append(hop(after(v, first[-1]) if k > 2 else v, k * PLANE))
        slots = []
        for k, s in enumerate(first):
            x, y = hop(s, 2), hop(s, 4)
            far = hop(x, 4) if k % 2 == 0 else hop(y, 2)
            slots.append(jnp.concatenate([s, x, y, far]))
        return slots

    def body(hidden, residual, down_weight, gain, proj_weight, centroids):
        me = lax.axis_index("dp")
        line, quad, core = me // PLANE, (me // 2) % QUAD, me % 2
        rows, hid = hidden.shape
        share = hid // n
        width = proj_weight.shape[1]
        cents = centroids.shape[0]

        orders = [[z] + [e[2] for e in table[z]] for z in range(lines)]
        place = jnp.array([[order.index(z) for z in range(lines)] for order in orders], jnp.int32)[line]
        d = jnp.arange(n)
        position = (((d // 2 % QUAD) ^ quad) * lines + place[d // PLANE]) * 2 + ((d % 2) ^ core)
        blocks = deal(hidden, position.astype(jnp.int32)).reshape(QUAD, lines, 2, rows, share)
        units = [blocks[0]] + [hop(blocks[k], 2 * k) for k in range(1, QUAD - 1)]

        down_rows = lax.all_to_all(down_weight, "dp", 0, 1, tiled=True)
        own = gain[:, None] * proj_weight.astype(F32)
        full = lax.all_gather(own, "cent", axis=0, tiled=True)
        high = lax.reduce_precision(full, 8, 7)
        low = (full - high).astype(BF16)
        high = high.astype(BF16)
        direct = dot(residual, own.astype(BF16))
        pair = jnp.concatenate([centroids, hop(centroids, 1)])
        down_rows, high, low, direct, pair, blocks = lax.optimization_barrier(
            (down_rows, high, low, direct, pair, blocks)
        )
        fold = (dot(down_rows, high) + dot(down_rows, low)).astype(BF16)
        fold, last = lax.optimization_barrier((fold, blocks[QUAD - 1]))
        units.append(hop(last, 2 * (QUAD - 1)))

        moved = {(0, 0): fold, (0, 1): fold}
        for s in range(1, lines):
            below, above = moved[s - 1, 0], moved[s - 1, 1]
            if s == lines - 1:
                below, above, units[-1] = lax.optimization_barrier((below, above, units[-1]))
            moved[s, 0], moved[s, 1] = up(below), down(above)
        folds = [fold]
        for s in range(lines - 1):
            folds.append(choose(line, [moved[table[z][s][:2]] for z in range(lines)]))
        units = jnp.concatenate(units, axis=2)
        part = 0.0
        for j, block in enumerate(folds):
            part = part + dot(units[j, 0], block) + dot(units[j, 1], hop(block, 1))
        part = part.reshape(QUAD, rows, width)

        raw = part[0] + direct
        for k in range(1, QUAD):
            raw = raw + hop(part[k].astype(BF16), 2 * k).astype(F32)
        raw = lax.psum(raw, "cent")
        embed = (raw * lax.rsqrt(jnp.mean(raw * raw, axis=1, keepdims=True) + 1e-06)).astype(BF16)

        inverse = 1.0 / (math.sqrt(width) * 0.05)
        slots = gather(embed)
        scores, local = [], []
        for block in slots:
            s = lax.dot_general(pair, block, (((1,), (1,)), ((), ())), preferred_element_type=F32)
            s = s * inverse
            top = jnp.max(s, axis=0, keepdims=True)
            scores.append(s)
            local.append(top + jnp.log(jnp.sum(jnp.exp(s - top), axis=0, keepdims=True)))

        v = jnp.concatenate(local).reshape(lines, QUAD, rows)
        got = [v] + [hop(v, 2 * k) for k in range(1, QUAD)]
        v = lse([jnp.stack([g[:, j ^ k] for j in range(QUAD)], axis=1) for k, g in enumerate(got)])
        got = [v] + [hop(v, PLANE * k) for k in range(1, lines)]
        v = lse([jnp.stack([g[j ^ k] for j in range(lines)]) for k, g in enumerate(got)])
        if lax.axis_size("cent") > 1:
            top = lax.pmax(v, "cent")
            v = top + jnp.log(lax.psum(jnp.exp(v - top), "cent"))
        totals = [v[k].reshape(1, QUAD * rows) for k in range(lines)]

        scale_up = cents * n * lax.axis_size("cent") / (rows * n)
        far, far_counts = weigh(scores, totals, slots, cents, cents, BF16, scale_up)
        near, near_counts = weigh(scores, totals, slots, 0, cents, F32, scale_up)
        weighted = scale_up * (near + hop(far, 1).astype(F32))
        counts = scale_up * (near_counts[:, 0] + hop(far_counts[:, 0], 1))
        return weighted, counts

    return body


def solution(mesh):
    n = mesh.shape["dp"]
    in_specs = (
        P("dp", "cent"),
        P("dp", "cent"),
        P("cent", "dp"),
        P("cent"),
        P("cent", None),
        P(("dp", "cent"), None),
    )
    out_specs = (P(("dp", "cent"), None), P(("dp", "cent")))
    return jax.shard_map(
        make_body(n, n // PLANE), mesh=mesh, in_specs=in_specs, out_specs=out_specs, check_vma=False
    )
```

```python
import math

import jax
import jax.numpy as jnp
from jax import lax
from jax.experimental import pallas as pl
from jax.experimental.pallas import tpu as pltpu
from jax.sharding import PartitionSpec as P


F32 = jnp.float32
BF16 = jnp.bfloat16
PLANE = 8
QUAD = 4


def dot(a, b):
    return jnp.dot(a, b, preferred_element_type=F32)


def after(v, *others):
    return lax.optimization_barrier((v, *others))[0]


def lse(parts):
    top = parts[0]
    for p in parts[1:]:
        top = jnp.maximum(top, p)
    return top + jnp.log(sum(jnp.exp(p - top) for p in parts))


def score_kernel(inverse, pair, *refs):
    blocks, (e, top, total) = refs[:-3], refs[-3:]
    x = jnp.concatenate([b[...] for b in blocks])
    s = lax.dot_general(pair[...], x, (((1,), (1,)), ((), ())), preferred_element_type=F32) * inverse
    most = jnp.max(s, axis=0, keepdims=True)
    weight = jnp.exp(s - most)
    e[...] = weight.astype(BF16)
    top[...] = most
    total[...] = most + jnp.log(jnp.sum(weight, axis=0, keepdims=True))


def score(pair, blocks):
    cents, width = pair.shape
    count = sum(b.shape[0] for b in blocks)
    return pl.pallas_call(
        lambda *refs: score_kernel(1.0 / (math.sqrt(width) * 0.05), *refs),
        out_shape=[
            jax.ShapeDtypeStruct((cents, count), BF16),
            jax.ShapeDtypeStruct((1, count), F32),
            jax.ShapeDtypeStruct((1, count), F32),
        ],
        compiler_params=pltpu.CompilerParams(vmem_limit_bytes=40 * 2**20),
        cost_estimate=pl.CostEstimate(
            flops=2 * cents * count * width,
            bytes_accessed=2 * (cents * width + count * width + cents * count),
            transcendentals=cents * count,
        ),
    )(pair, *blocks)


def weigh_kernel(sizes, scale, *refs):
    count, pieces = len(sizes), sum(len(s) for s in sizes)
    ws, es, blocks = refs[:count], refs[count : 2 * count], refs[2 * count : 2 * count + pieces]
    near, far, counts, *scratch = refs[2 * count + pieces :]
    xs, ps, total, sems = scratch[:count], scratch[count : 2 * count], scratch[-2], scratch[-1]
    blocks = list(blocks)
    copies = []
    for g, group in enumerate(sizes):
        copies.append([pltpu.make_async_copy(es[g], ps[g], sems.at[len(sems_of(sizes, g))])])
        at = 0
        for k, size in enumerate(group):
            sem = sems.at[len(sems_of(sizes, g)) + 1 + k]
            copies[-1].append(pltpu.make_async_copy(blocks.pop(0), xs[g].at[pl.ds(at, size)], sem))
            at += size
    for group in copies[:2]:
        for copy in group:
            copy.start()
    masses = 0.0
    for g in range(count):
        copies[g][0].wait()
        prob = ps[g][...].astype(F32) * ws[g][...]
        masses = masses + jnp.sum(prob, axis=1, keepdims=True)
        for copy in copies[g][1:]:
            copy.wait()
        if g + 2 < count:
            for copy in copies[g + 2]:
                copy.start()
        term = dot(prob.astype(BF16), xs[g][...])
        total[...] = term if g == 0 else total[...] + term
    cents = near.shape[0]
    near[...] = total[:cents] * scale
    far[...] = (total[cents:] * scale).astype(BF16)
    counts[...] = masses * scale


def sems_of(sizes, g):
    return [s for group in sizes[:g] for s in (0, *group)]


def weigh(groups, es, ws, scale):
    sizes = [[b.shape[0] for b in group] for group in groups]
    width = groups[0][0].shape[1]
    cents = es[0].shape[0]
    some = pl.BlockSpec(memory_space=pl.ANY)
    blocks = [b for group in groups for b in group]
    passages = sum(b.shape[0] for b in blocks)
    return pl.pallas_call(
        lambda *refs: weigh_kernel(sizes, scale, *refs),
        in_specs=[pl.BlockSpec(w.shape, lambda: (0, 0)) for w in ws] + [some] * (len(es) + len(blocks)),
        out_shape=[
            jax.ShapeDtypeStruct((cents // 2, width), F32),
            jax.ShapeDtypeStruct((cents // 2, width), BF16),
            jax.ShapeDtypeStruct((cents, 1), F32),
        ],
        scratch_shapes=[pltpu.VMEM((sum(s), width), BF16) for s in sizes]
        + [pltpu.VMEM((cents, sum(s)), BF16) for s in sizes]
        + [pltpu.VMEM((cents, width), F32), pltpu.SemaphoreType.DMA((len(sems_of(sizes, len(sizes))),))],
        compiler_params=pltpu.CompilerParams(vmem_limit_bytes=56 * 2**20),
        cost_estimate=pl.CostEstimate(
            flops=2 * cents * passages * width,
            bytes_accessed=2 * passages * (cents + width) + 8 * cents * width,
            transcendentals=0,
        ),
    )(*ws, *es, *blocks)


def deal_kernel(position, hidden, blocks):
    share = blocks.shape[2]
    for d in range(blocks.shape[0]):
        blocks[position[d]] = hidden[:, d * share : (d + 1) * share]


def deal(hidden, position):
    rows, hid = hidden.shape
    n = position.shape[0]
    vmem = pl.BlockSpec(memory_space=pltpu.VMEM)
    return pl.pallas_call(
        deal_kernel,
        in_specs=[pl.BlockSpec(memory_space=pltpu.SMEM), vmem],
        out_specs=vmem,
        out_shape=jax.ShapeDtypeStruct((n, rows, hid // n), hidden.dtype),
        compiler_params=pltpu.CompilerParams(vmem_limit_bytes=32 * 2**20),
        cost_estimate=pl.CostEstimate(flops=0, bytes_accessed=4 * rows * hid, transcendentals=0),
    )(position, hidden)


def arrivals(lines):
    table = []
    for z in range(lines):
        near = [(s, w, z - s if w == 0 else z + s) for s in range(1, lines) for w in (1, 0)]
        table.append([e for e in near if 0 <= e[2] < lines])
    return table


def make_body(n, lines):
    table = arrivals(lines)

    def hop(v, k):
        return lax.ppermute(v, "dp", [(i, i ^ k) for i in range(n)])

    def up(v):
        return lax.ppermute(v, "dp", [(i, i + PLANE) for i in range(n - PLANE)])

    def down(v):
        return lax.ppermute(v, "dp", [(i + PLANE, i) for i in range(n - PLANE)])

    def choose(line, values):
        out = values[-1]
        for z in range(lines - 2, -1, -1):
            if values[z] is not out:
                out = jnp.where(line <= z, values[z], out)
        return out

    def along(v):
        line = lax.axis_index("dp") // PLANE
        moved = {(0, 0): v, (0, 1): v}
        block = v
        for s in range(1, lines):
            ties = yield block
            below, above = moved[s - 1, 0], moved[s - 1, 1]
            if ties:
                below, above, *_ = lax.optimization_barrier((below, above, *ties))
            moved[s, 0], moved[s, 1] = up(below), down(above)
            block = choose(line, [moved[table[z][s - 1][:2]] for z in range(lines)])
        yield block

    def body(hidden, residual, down_weight, gain, proj_weight, centroids):
        me = lax.axis_index("dp")
        line, quad, core = me // PLANE, (me // 2) % QUAD, me % 2
        rows, hid = hidden.shape
        share = hid // n
        width = proj_weight.shape[1]
        cents = centroids.shape[0]

        orders = [[z] + [e[2] for e in table[z]] for z in range(lines)]
        place = jnp.array([[order.index(z) for z in range(lines)] for order in orders], jnp.int32)[line]
        d = jnp.arange(n)
        position = (((d // 2 % QUAD) ^ quad) * lines + place[d // PLANE]) * 2 + ((d % 2) ^ core)
        blocks = deal(hidden, position.astype(jnp.int32)).reshape(QUAD, lines, 2, rows, share)
        units = [blocks[0]] + [hop(blocks[k], 2 * k) for k in range(1, QUAD - 1)]

        down_rows = lax.all_to_all(down_weight, "dp", 0, 1, tiled=True)
        own = gain[:, None] * proj_weight.astype(F32)
        full = lax.all_gather(own, "cent", axis=0, tiled=True)
        high = lax.reduce_precision(full, 8, 7)
        low = (full - high).astype(BF16)
        high = high.astype(BF16)
        direct = dot(residual, own.astype(BF16))
        pair = jnp.concatenate([centroids, hop(centroids, 1)])
        down_rows, high, low, direct, pair, blocks, *units = lax.optimization_barrier(
            (down_rows, high, low, direct, pair, blocks, *units)
        )
        fold = (dot(down_rows, high) + dot(down_rows, low)).astype(BF16)
        fold, last = lax.optimization_barrier((fold, blocks[QUAD - 1]))
        units.append(hop(last, 2 * (QUAD - 1)))

        units = jnp.concatenate(units, axis=2)
        steps = along(fold)
        part = 0.0
        for j in range(lines):
            block = next(steps) if j == 0 else steps.send(None)
            part = part + dot(units[j, 0], block) + dot(units[j, 1], hop(block, 1))
        part = part.reshape(QUAD, rows, width)

        raw = part[0] + direct
        for k in range(1, QUAD):
            raw = raw + hop(part[k].astype(BF16), 2 * k).astype(F32)
        raw = lax.psum(raw, "cent")
        embed = (raw * lax.rsqrt(jnp.mean(raw * raw, axis=1, keepdims=True) + 1e-06)).astype(BF16)

        def spread(block):
            return [block, hop(block, 2), hop(block, 4)]

        scale_up = cents * n * lax.axis_size("cent") / (rows * n)
        groups, tags, scored = [], [], []

        def take(blocks, names):
            groups.append(blocks)
            tags.append(names)
            scored.append(score(pair, blocks))

        first = spread(embed)
        lined = [None] + [hop(embed if k < 3 else after(embed, first[1]), k * PLANE) for k in range(1, lines)]
        take(first + [hop(first[1], 4)], [(0, q) for q in (0, 1, 2, 3)])
        late, late_names, ends, end_names = [], [], [], []
        for k in range(1, lines):
            wait = scored[k // 2 - 1][2] if k % 2 == 0 else scored[0][2] if k > 1 else None
            got = spread(lined[k] if wait is None else after(lined[k], wait))
            names = [(k, 0), (k, 1), (k, 2)]
            end = (2, 1) if k % 2 == 1 else (1, 2)
            start = got[end[0]]
            if k == 1:
                take(got + [hop(start, 2 * end[1])], names + [(k, 3)])
            else:
                late, late_names = late + got, late_names + names
                ends.append(hop(after(start, scored[1][2]), 2 * end[1]))
                end_names.append((k, 3))
        take(late, late_names)
        ends = lax.optimization_barrier((*ends, scored[-1][2]))[:-1]
        take(list(ends), end_names)

        parts = {}
        for names, (_, _, total) in zip(tags, scored):
            for i, name in enumerate(names):
                parts[name] = total[:, i * rows : (i + 1) * rows]
        v = jnp.stack([jnp.concatenate([parts[k, q] for q in range(QUAD)]) for k in range(lines)])
        got = [v] + [hop(v, 2 * k) for k in range(1, QUAD)]
        v = lse([jnp.stack([g[:, j ^ k] for j in range(QUAD)], axis=1) for k, g in enumerate(got)])
        got = [v] + [hop(v, PLANE * k) for k in range(1, lines)]
        v = lse([jnp.stack([g[j ^ k] for j in range(lines)]) for k, g in enumerate(got)])
        if lax.axis_size("cent") > 1:
            top = lax.pmax(v, "cent")
            v = top + jnp.log(lax.psum(jnp.exp(v - top), "cent"))
        ws = []
        for names, (_, top, _) in zip(tags, scored):
            ws.append(jnp.exp(top - jnp.concatenate([v[k, q] for k, q in names])[None]))

        near, far, masses = weigh(groups, [e for e, _, _ in scored], ws, scale_up)
        weighted = near + hop(far, 1).astype(F32)
        counts = masses[:cents, 0] + hop(masses[cents:, 0], 1)
        return weighted, counts

    return body


def solution(mesh):
    n = mesh.shape["dp"]
    in_specs = (
        P("dp", "cent"),
        P("dp", "cent"),
        P("cent", "dp"),
        P("cent"),
        P("cent", None),
        P(("dp", "cent"), None),
    )
    out_specs = (P(("dp", "cent"), None), P(("dp", "cent")))
    return jax.shard_map(
        make_body(n, n // PLANE), mesh=mesh, in_specs=in_specs, out_specs=out_specs, check_vma=False
    )
```

```python
import math

import jax
import jax.numpy as jnp
from jax import lax
from jax.experimental import pallas as pl
from jax.experimental.pallas import tpu as pltpu
from jax.sharding import PartitionSpec as P


F32 = jnp.float32
BF16 = jnp.bfloat16
PLANE = 8
QUAD = 4


def dot(a, b):
    return jnp.dot(a, b, preferred_element_type=F32)


def after(v, *others):
    return lax.optimization_barrier((v, *others))[0]


def lse(parts):
    top = parts[0]
    for p in parts[1:]:
        top = jnp.maximum(top, p)
    return top + jnp.log(sum(jnp.exp(p - top) for p in parts))


def padded(size):
    return -(-size // 128) * 128


def score_kernel(inverse, pair, *refs):
    blocks, (e, top, total) = refs[:-3], refs[-3:]
    count = sum(b.shape[0] for b in blocks)
    rest = jnp.zeros((e.shape[1] - count, pair.shape[1]), BF16)
    x = jnp.concatenate([b[...] for b in blocks] + [rest])
    s = lax.dot_general(pair[...], x, (((1,), (1,)), ((), ())), preferred_element_type=F32) * inverse
    most = jnp.max(s, axis=0, keepdims=True)
    weight = jnp.exp(s - most)
    column = lax.broadcasted_iota(jnp.int32, weight.shape, 1)
    e[...] = jnp.where(column < count, weight, 0.0).astype(BF16)
    top[...] = most
    total[...] = most + jnp.log(jnp.sum(weight, axis=0, keepdims=True))


def score(pair, blocks):
    cents, width = pair.shape
    count = padded(sum(b.shape[0] for b in blocks))
    return pl.pallas_call(
        lambda *refs: score_kernel(1.0 / (math.sqrt(width) * 0.05), *refs),
        out_shape=[
            jax.ShapeDtypeStruct((cents, count), BF16),
            jax.ShapeDtypeStruct((1, count), F32),
            jax.ShapeDtypeStruct((1, count), F32),
        ],
        compiler_params=pltpu.CompilerParams(vmem_limit_bytes=40 * 2**20),
        cost_estimate=pl.CostEstimate(
            flops=2 * cents * count * width,
            bytes_accessed=2 * (cents * width + count * width + cents * count),
            transcendentals=cents * count,
        ),
    )(pair, *blocks)


def weigh_kernel(sizes, scale, w, *refs):
    count, pieces = len(sizes), sum(len(s) for s in sizes)
    es, blocks = refs[:count], list(refs[count : count + pieces])
    near, far, counts, x, p, sems = refs[count + pieces :]
    cents = near.shape[0]
    copies, spans, sem, start = [], [], 0, 0
    for e, group in zip(es, sizes):
        stop = start + e.shape[1]
        spans.append(slice(start, stop))
        copies.append([pltpu.make_async_copy(e, p.at[:, pl.ds(start, e.shape[1])], sems.at[sem])])
        sem += 1
        for size in group:
            copies[-1].append(pltpu.make_async_copy(blocks.pop(0), x.at[pl.ds(start, size)], sems.at[sem]))
            sem += 1
            start += size
        if start < stop:
            x[start:stop] = jnp.zeros((stop - start, x.shape[1]), BF16)
        start = stop
    for group in copies:
        for copy in group:
            copy.start()
    for group in copies:
        for copy in group:
            copy.wait()
    for rows, out in ((slice(cents, 2 * cents), far), (slice(0, cents), near)):
        masses = 0.0
        for span in spans:
            prob = p[rows, span].astype(F32) * w[:, span]
            masses = masses + jnp.sum(prob, axis=1, keepdims=True)
            p[rows, span] = prob.astype(BF16)
        counts[rows] = masses * scale
        out[...] = (dot(p[rows], x[...]) * scale).astype(out.dtype)


def weigh(groups, es, w, scale):
    sizes = [[b.shape[0] for b in group] for group in groups]
    width = groups[0][0].shape[1]
    cents = es[0].shape[0]
    passages = sum(e.shape[1] for e in es)
    some = pl.BlockSpec(memory_space=pl.ANY)
    blocks = [b for group in groups for b in group]
    return pl.pallas_call(
        lambda *refs: weigh_kernel(sizes, scale, *refs),
        in_specs=[pl.BlockSpec(w.shape, lambda: (0, 0))] + [some] * (len(es) + len(blocks)),
        out_shape=[
            jax.ShapeDtypeStruct((cents // 2, width), F32),
            jax.ShapeDtypeStruct((cents // 2, width), BF16),
            jax.ShapeDtypeStruct((cents, 1), F32),
        ],
        scratch_shapes=[
            pltpu.VMEM((passages, width), BF16),
            pltpu.VMEM((cents, passages), BF16),
            pltpu.SemaphoreType.DMA((len(es) + len(blocks),)),
        ],
        compiler_params=pltpu.CompilerParams(vmem_limit_bytes=56 * 2**20),
        cost_estimate=pl.CostEstimate(
            flops=2 * cents * passages * width,
            bytes_accessed=2 * passages * (cents + width) + 8 * cents * width,
            transcendentals=0,
        ),
    )(w, *es, *blocks)


def deal_kernel(position, hidden, blocks):
    share = blocks.shape[2]
    for d in range(blocks.shape[0]):
        blocks[position[d]] = hidden[:, d * share : (d + 1) * share]


def deal(hidden, position):
    rows, hid = hidden.shape
    n = position.shape[0]
    vmem = pl.BlockSpec(memory_space=pltpu.VMEM)
    return pl.pallas_call(
        deal_kernel,
        in_specs=[pl.BlockSpec(memory_space=pltpu.SMEM), vmem],
        out_specs=vmem,
        out_shape=jax.ShapeDtypeStruct((n, rows, hid // n), hidden.dtype),
        compiler_params=pltpu.CompilerParams(vmem_limit_bytes=32 * 2**20),
        cost_estimate=pl.CostEstimate(flops=0, bytes_accessed=4 * rows * hid, transcendentals=0),
    )(position, hidden)


def arrivals(lines):
    table = []
    for z in range(lines):
        near = [(s, w, z - s if w == 0 else z + s) for s in range(1, lines) for w in (1, 0)]
        table.append([e for e in near if 0 <= e[2] < lines])
    return table


def make_body(n, lines):
    table = arrivals(lines)

    def hop(v, k):
        return lax.ppermute(v, "dp", [(i, i ^ k) for i in range(n)])

    def up(v):
        return lax.ppermute(v, "dp", [(i, i + PLANE) for i in range(n - PLANE)])

    def down(v):
        return lax.ppermute(v, "dp", [(i + PLANE, i) for i in range(n - PLANE)])

    def choose(line, values):
        out = values[-1]
        for z in range(lines - 2, -1, -1):
            if values[z] is not out:
                out = jnp.where(line <= z, values[z], out)
        return out

    def along(v):
        line = lax.axis_index("dp") // PLANE
        moved = {(0, 0): v, (0, 1): v}
        block = v
        for s in range(1, lines):
            ties = yield block
            below, above = moved[s - 1, 0], moved[s - 1, 1]
            if ties:
                below, above, *_ = lax.optimization_barrier((below, above, *ties))
            moved[s, 0], moved[s, 1] = up(below), down(above)
            block = choose(line, [moved[table[z][s - 1][:2]] for z in range(lines)])
        yield block

    def body(hidden, residual, down_weight, gain, proj_weight, centroids):
        me = lax.axis_index("dp")
        line, quad, core = me // PLANE, (me // 2) % QUAD, me % 2
        rows, hid = hidden.shape
        share = hid // n
        width = proj_weight.shape[1]
        cents = centroids.shape[0]

        orders = [[z] + [e[2] for e in table[z]] for z in range(lines)]
        place = jnp.array([[order.index(z) for z in range(lines)] for order in orders], jnp.int32)[line]
        d = jnp.arange(n)
        position = (((d // 2 % QUAD) ^ quad) * lines + place[d // PLANE]) * 2 + ((d % 2) ^ core)
        blocks = deal(hidden, position.astype(jnp.int32)).reshape(QUAD, lines, 2, rows, share)
        units = [blocks[0]] + [hop(blocks[k], 2 * k) for k in range(1, QUAD - 1)]

        down_rows = lax.all_to_all(down_weight, "dp", 0, 1, tiled=True)
        own = gain[:, None] * proj_weight.astype(F32)
        full = lax.all_gather(own, "cent", axis=0, tiled=True)
        high = lax.reduce_precision(full, 8, 7)
        low = (full - high).astype(BF16)
        high = high.astype(BF16)
        direct = dot(residual, own.astype(BF16))
        pair = jnp.concatenate([centroids, hop(centroids, 1)])
        last = blocks[QUAD - 1]
        down_rows, high, low, direct, pair, last, *units = lax.optimization_barrier(
            (down_rows, high, low, direct, pair, last, *units)
        )

        halves = [slice(0, width // 2), slice(width // 2, width)]
        folds = []
        for h in halves:
            source = after(down_rows, folds[0]) if folds else down_rows
            folds.append((dot(source, high[:, h]) + dot(source, low[:, h])).astype(BF16))
            if not units[QUAD - 1 :]:
                last, folds[0] = lax.optimization_barrier((last, folds[0]))
                units.append(hop(last, 2 * (QUAD - 1)))
        units = jnp.concatenate(units, axis=2)
        walks = [along(f) for f in folds]
        parts = [0.0, 0.0]
        for j in range(lines):
            for i, walk in enumerate(walks):
                block = next(walk) if j == 0 else walk.send(None)
                parts[i] = parts[i] + dot(units[j, 0], block) + dot(units[j, 1], hop(block, 1))
        raws = []
        for h, part in zip(halves, parts):
            part = part.reshape(QUAD, rows, -1)
            raw = part[0] + direct[:, h]
            for k in range(1, QUAD):
                raw = raw + hop(part[k].astype(BF16), 2 * k).astype(F32)
            raws.append(raw)
        raw = jnp.concatenate(raws, axis=1)
        raw = lax.psum(raw, "cent")
        embed = (raw * lax.rsqrt(jnp.mean(raw * raw, axis=1, keepdims=True) + 1e-06)).astype(BF16)

        def spread(block):
            return [block, hop(block, 2), hop(block, 4)]

        scale_up = cents * n * lax.axis_size("cent") / (rows * n)
        groups, tags, scored = [], [], []

        def take(blocks, names):
            groups.append(blocks)
            tags.append(names)
            scored.append(score(pair, blocks))

        first = spread(embed)
        lined = [None] + [hop(embed if k < 3 else after(embed, first[1]), k * PLANE) for k in range(1, lines)]
        take(first + [hop(first[1], 4)], [(0, q) for q in (0, 1, 2, 3)])
        late, late_names, ends, end_names = [], [], [], []
        for k in range(1, lines):
            wait = scored[k // 2 - 1][2] if k % 2 == 0 else scored[0][2] if k > 1 else None
            got = spread(lined[k] if wait is None else after(lined[k], wait))
            names = [(k, 0), (k, 1), (k, 2)]
            end = (2, 1) if k % 2 == 1 else (1, 2)
            start = got[end[0]]
            if k == 1:
                take(got + [hop(start, 2 * end[1])], names + [(k, 3)])
            else:
                late, late_names = late + got, late_names + names
                ends.append(hop(after(start, scored[1][2]), 2 * end[1]))
                end_names.append((k, 3))
        take(late, late_names)
        ends = lax.optimization_barrier((*ends, scored[-1][2]))[:-1]
        take(list(ends), end_names)

        parts = {}
        for names, (_, _, total) in zip(tags, scored):
            for i, name in enumerate(names):
                parts[name] = total[:, i * rows : (i + 1) * rows]
        v = jnp.stack([jnp.concatenate([parts[k, q] for q in range(QUAD)]) for k in range(lines)])
        got = [v] + [hop(v, 2 * k) for k in range(1, QUAD)]
        v = lse([jnp.stack([g[:, j ^ k] for j in range(QUAD)], axis=1) for k, g in enumerate(got)])
        got = [v] + [hop(v, PLANE * k) for k in range(1, lines)]
        v = lse([jnp.stack([g[j ^ k] for j in range(lines)]) for k, g in enumerate(got)])
        if lax.axis_size("cent") > 1:
            top = lax.pmax(v, "cent")
            v = top + jnp.log(lax.psum(jnp.exp(v - top), "cent"))
        tops = jnp.concatenate([top for _, top, _ in scored], axis=1)
        logs = []
        for names, (_, top, _) in zip(tags, scored):
            logs += [v[k, q] for k, q in names]
            logs.append(jnp.zeros(top.shape[1] - len(names) * rows, F32))
        w = jnp.exp(tops - jnp.concatenate(logs)[None])

        near, far, masses = weigh(groups, [e for e, _, _ in scored], w, scale_up)
        weighted = near + hop(far, 1).astype(F32)
        counts = masses[:cents, 0] + hop(masses[cents:, 0], 1)
        return weighted, counts

    return body


def solution(mesh):
    n = mesh.shape["dp"]
    in_specs = (
        P("dp", "cent"),
        P("dp", "cent"),
        P("cent", "dp"),
        P("cent"),
        P("cent", None),
        P(("dp", "cent"), None),
    )
    out_specs = (P(("dp", "cent"), None), P(("dp", "cent")))
    return jax.shard_map(
        make_body(n, n // PLANE), mesh=mesh, in_specs=in_specs, out_specs=out_specs, check_vma=False
    )
```

```python
import math

import jax
import jax.numpy as jnp
from jax import lax
from jax.experimental import pallas as pl
from jax.experimental.pallas import tpu as pltpu
from jax.sharding import PartitionSpec as P


F32 = jnp.float32
BF16 = jnp.bfloat16
PLANE = 8
QUAD = 4


def dot(a, b):
    return jnp.dot(a, b, preferred_element_type=F32)


def after(v, *others):
    return lax.optimization_barrier((v, *others))[0]


def lse(parts):
    top = parts[0]
    for p in parts[1:]:
        top = jnp.maximum(top, p)
    return top + jnp.log(sum(jnp.exp(p - top) for p in parts))


def padded(size):
    return -(-size // 128) * 128


def score_kernel(inverse, pair, *refs):
    blocks, (e, top, total) = refs[:-3], refs[-3:]
    count = sum(b.shape[0] for b in blocks)
    rest = jnp.zeros((e.shape[1] - count, pair.shape[1]), BF16)
    x = jnp.concatenate([b[...] for b in blocks] + [rest])
    s = lax.dot_general(pair[...], x, (((1,), (1,)), ((), ())), preferred_element_type=F32) * inverse
    most = jnp.max(s, axis=0, keepdims=True)
    weight = jnp.exp(s - most)
    column = lax.broadcasted_iota(jnp.int32, weight.shape, 1)
    e[...] = jnp.where(column < count, weight, 0.0).astype(BF16)
    top[...] = most
    total[...] = most + jnp.log(jnp.sum(weight, axis=0, keepdims=True))


def score(pair, blocks):
    cents, width = pair.shape
    count = padded(sum(b.shape[0] for b in blocks))
    return pl.pallas_call(
        lambda *refs: score_kernel(1.0 / (math.sqrt(width) * 0.05), *refs),
        out_shape=[
            jax.ShapeDtypeStruct((cents, count), BF16),
            jax.ShapeDtypeStruct((1, count), F32),
            jax.ShapeDtypeStruct((1, count), F32),
        ],
        compiler_params=pltpu.CompilerParams(vmem_limit_bytes=40 * 2**20),
        cost_estimate=pl.CostEstimate(
            flops=2 * cents * count * width,
            bytes_accessed=2 * (cents * width + count * width + cents * count),
            transcendentals=cents * count,
        ),
    )(pair, *blocks)


def weigh_kernel(sizes, scale, tiles, w, *refs):
    count, pieces = len(sizes), sum(len(s) for s in sizes)
    es, blocks = refs[:count], list(refs[count : count + pieces])
    near, far, counts, x, p = refs[count + pieces :]
    step = pl.program_id(0)

    @pl.when(step == 0)
    def _():
        at = 0
        for e, group in zip(es, sizes):
            stop = at + e.shape[1]
            for size in group:
                x[at : at + size] = blocks.pop(0)[...]
                at += size
            if at < stop:
                x[at:stop] = jnp.zeros((stop - at, x.shape[1]), BF16)
            at = stop

    at, masses = 0, 0.0
    for e in es:
        span = slice(at, at + e.shape[1])
        prob = e[...].astype(F32) * w[:, span]
        masses = masses + jnp.sum(prob, axis=1, keepdims=True)
        p[:, span] = prob.astype(BF16)
        at = span.stop
    counts[...] = jnp.transpose(jnp.broadcast_to(masses * scale, (masses.shape[0], 128)))[:1]
    sums = dot(p[...], x[...]) * scale

    @pl.when(step < tiles)
    def _():
        far[...] = sums.astype(BF16)

    @pl.when(step >= tiles)
    def _():
        near[...] = sums


def weigh(groups, es, w, scale):
    sizes = [[b.shape[0] for b in group] for group in groups]
    blocks = [b for group in groups for b in group]
    width = blocks[0].shape[1]
    cents = es[0].shape[0]
    passages = sum(e.shape[1] for e in es)
    tile = math.gcd(cents // 2, 256)
    tiles = cents // 2 // tile
    turn = lambda i: (i + tiles) % (2 * tiles)
    whole = lambda b: pl.BlockSpec(b.shape, lambda i: (0, 0), pipeline_mode=pl.Buffered(1))
    return pl.pallas_call(
        lambda *refs: weigh_kernel(sizes, scale, tiles, *refs),
        grid=(2 * tiles,),
        in_specs=[whole(w)]
        + [pl.BlockSpec((tile, e.shape[1]), lambda i: (turn(i), 0)) for e in es]
        + [whole(b) for b in blocks],
        out_specs=[
            pl.BlockSpec((tile, width), lambda i: (jnp.maximum(i - tiles, 0), 0)),
            pl.BlockSpec((tile, width), lambda i: (jnp.minimum(i, tiles - 1), 0)),
            pl.BlockSpec((1, tile), lambda i: (0, turn(i))),
        ],
        out_shape=[
            jax.ShapeDtypeStruct((cents // 2, width), F32),
            jax.ShapeDtypeStruct((cents // 2, width), BF16),
            jax.ShapeDtypeStruct((1, cents), F32),
        ],
        scratch_shapes=[pltpu.VMEM((passages, width), BF16), pltpu.VMEM((tile, passages), BF16)],
        compiler_params=pltpu.CompilerParams(vmem_limit_bytes=56 * 2**20),
        cost_estimate=pl.CostEstimate(
            flops=2 * cents * passages * width,
            bytes_accessed=2 * passages * (cents + width) + 8 * cents * width,
            transcendentals=0,
        ),
    )(w, *es, *blocks)


def deal_kernel(position, hidden, blocks):
    share = blocks.shape[2]
    for d in range(blocks.shape[0]):
        blocks[position[d]] = hidden[:, d * share : (d + 1) * share]


def deal(hidden, position):
    rows, hid = hidden.shape
    n = position.shape[0]
    vmem = pl.BlockSpec(memory_space=pltpu.VMEM)
    return pl.pallas_call(
        deal_kernel,
        in_specs=[pl.BlockSpec(memory_space=pltpu.SMEM), vmem],
        out_specs=vmem,
        out_shape=jax.ShapeDtypeStruct((n, rows, hid // n), hidden.dtype),
        compiler_params=pltpu.CompilerParams(vmem_limit_bytes=32 * 2**20),
        cost_estimate=pl.CostEstimate(flops=0, bytes_accessed=4 * rows * hid, transcendentals=0),
    )(position, hidden)


def arrivals(lines):
    table = []
    for z in range(lines):
        near = [(s, w, z - s if w == 0 else z + s) for s in range(1, lines) for w in (1, 0)]
        table.append([e for e in near if 0 <= e[2] < lines])
    return table


def make_body(n, lines):
    table = arrivals(lines)

    def hop(v, k):
        return lax.ppermute(v, "dp", [(i, i ^ k) for i in range(n)])

    def up(v):
        return lax.ppermute(v, "dp", [(i, i + PLANE) for i in range(n - PLANE)])

    def down(v):
        return lax.ppermute(v, "dp", [(i + PLANE, i) for i in range(n - PLANE)])

    def choose(line, values):
        out = values[-1]
        for z in range(lines - 2, -1, -1):
            if values[z] is not out:
                out = jnp.where(line <= z, values[z], out)
        return out

    def along(v):
        line = lax.axis_index("dp") // PLANE
        moved = {(0, 0): v, (0, 1): v}
        block = v
        for s in range(1, lines):
            ties = yield block
            below, above = moved[s - 1, 0], moved[s - 1, 1]
            if ties:
                below, above, *_ = lax.optimization_barrier((below, above, *ties))
            moved[s, 0], moved[s, 1] = up(below), down(above)
            block = choose(line, [moved[table[z][s - 1][:2]] for z in range(lines)])
        yield block

    def body(hidden, residual, down_weight, gain, proj_weight, centroids):
        me = lax.axis_index("dp")
        line, quad, core = me // PLANE, (me // 2) % QUAD, me % 2
        rows, hid = hidden.shape
        share = hid // n
        width = proj_weight.shape[1]
        cents = centroids.shape[0]

        orders = [[z] + [e[2] for e in table[z]] for z in range(lines)]
        place = jnp.array([[order.index(z) for z in range(lines)] for order in orders], jnp.int32)[line]
        d = jnp.arange(n)
        position = (((d // 2 % QUAD) ^ quad) * lines + place[d // PLANE]) * 2 + ((d % 2) ^ core)
        blocks = deal(hidden, position.astype(jnp.int32)).reshape(QUAD, lines, 2, rows, share)
        units = [blocks[0]] + [hop(blocks[k], 2 * k) for k in range(1, QUAD - 1)]

        down_rows = lax.all_to_all(down_weight, "dp", 0, 1, tiled=True)
        own = gain[:, None] * proj_weight.astype(F32)
        full = lax.all_gather(own, "cent", axis=0, tiled=True)
        high = lax.reduce_precision(full, 8, 7)
        low = (full - high).astype(BF16)
        high = high.astype(BF16)
        direct = dot(residual, own.astype(BF16))
        pair = jnp.concatenate([centroids, hop(centroids, 1)])
        last = blocks[QUAD - 1]
        down_rows, high, low, direct, pair, last, *units = lax.optimization_barrier(
            (down_rows, high, low, direct, pair, last, *units)
        )

        halves = [slice(0, width // 2), slice(width // 2, width)]
        folds = []
        for h in halves:
            source = after(down_rows, folds[0]) if folds else down_rows
            folds.append((dot(source, high[:, h]) + dot(source, low[:, h])).astype(BF16))
            if not units[QUAD - 1 :]:
                last, folds[0] = lax.optimization_barrier((last, folds[0]))
                units.append(hop(last, 2 * (QUAD - 1)))
        units = jnp.concatenate(units, axis=2)
        walks = [along(f) for f in folds]
        parts = [0.0, 0.0]
        for j in range(lines):
            for i, walk in enumerate(walks):
                block = next(walk) if j == 0 else walk.send(None)
                parts[i] = parts[i] + dot(units[j, 0], block) + dot(units[j, 1], hop(block, 1))
        raws = []
        for h, part in zip(halves, parts):
            part = part.reshape(QUAD, rows, -1)
            raw = part[0] + direct[:, h]
            for k in range(1, QUAD):
                raw = raw + hop(part[k].astype(BF16), 2 * k).astype(F32)
            raws.append(raw)
        raw = jnp.concatenate(raws, axis=1)
        raw = lax.psum(raw, "cent")
        embed = (raw * lax.rsqrt(jnp.mean(raw * raw, axis=1, keepdims=True) + 1e-06)).astype(BF16)

        def spread(block):
            return [block, hop(block, 2), hop(block, 4)]

        scale_up = cents * n * lax.axis_size("cent") / (rows * n)
        groups, tags, scored = [], [], []

        def take(blocks, names):
            groups.append(blocks)
            tags.append(names)
            scored.append(score(pair, blocks))

        first = spread(embed)
        lined = [None] + [hop(embed if k < 3 else after(embed, first[1]), k * PLANE) for k in range(1, lines)]
        take(first + [hop(first[1], 4)], [(0, q) for q in (0, 1, 2, 3)])
        late, late_names, ends, end_names = [], [], [], []
        for k in range(1, lines):
            wait = scored[k // 2 - 1][2] if k % 2 == 0 else scored[0][2] if k > 1 else None
            got = spread(lined[k] if wait is None else after(lined[k], wait))
            names = [(k, 0), (k, 1), (k, 2)]
            end = (2, 1) if k % 2 == 1 else (1, 2)
            start = got[end[0]]
            if k == 1:
                take(got + [hop(start, 2 * end[1])], names + [(k, 3)])
            else:
                late, late_names = late + got, late_names + names
                ends.append(hop(after(start, scored[1][2]), 2 * end[1]))
                end_names.append((k, 3))
        take(late, late_names)
        ends = lax.optimization_barrier((*ends, scored[-1][2]))[:-1]
        take(list(ends), end_names)

        parts = {}
        for names, (_, _, total) in zip(tags, scored):
            for i, name in enumerate(names):
                parts[name] = total[:, i * rows : (i + 1) * rows]
        v = jnp.stack([jnp.concatenate([parts[k, q] for q in range(QUAD)]) for k in range(lines)])
        got = [v] + [hop(v, 2 * k) for k in range(1, QUAD)]
        v = lse([jnp.stack([g[:, j ^ k] for j in range(QUAD)], axis=1) for k, g in enumerate(got)])
        got = [v] + [hop(v, PLANE * k) for k in range(1, lines)]
        v = lse([jnp.stack([g[j ^ k] for j in range(lines)]) for k, g in enumerate(got)])
        if lax.axis_size("cent") > 1:
            top = lax.pmax(v, "cent")
            v = top + jnp.log(lax.psum(jnp.exp(v - top), "cent"))
        tops = jnp.concatenate([top for _, top, _ in scored], axis=1)
        logs = []
        for names, (_, top, _) in zip(tags, scored):
            logs += [v[k, q] for k, q in names]
            logs.append(jnp.zeros(top.shape[1] - len(names) * rows, F32))
        w = jnp.exp(tops - jnp.concatenate(logs)[None])

        near, far, masses = weigh(groups, [e for e, _, _ in scored], w, scale_up)
        weighted = near + hop(far, 1).astype(F32)
        counts = masses[0, :cents] + hop(masses[0, cents:], 1)
        return weighted, counts

    return body


def solution(mesh):
    n = mesh.shape["dp"]
    in_specs = (
        P("dp", "cent"),
        P("dp", "cent"),
        P("cent", "dp"),
        P("cent"),
        P("cent", None),
        P(("dp", "cent"), None),
    )
    out_specs = (P(("dp", "cent"), None), P(("dp", "cent")))
    return jax.shard_map(
        make_body(n, n // PLANE), mesh=mesh, in_specs=in_specs, out_specs=out_specs, check_vma=False
    )
```

```python
import math

import jax
import jax.numpy as jnp
from jax import lax
from jax.experimental import pallas as pl
from jax.experimental.pallas import tpu as pltpu
from jax.sharding import PartitionSpec as P


F32 = jnp.float32
BF16 = jnp.bfloat16
PLANE = 8
QUAD = 4


def dot(a, b):
    return jnp.dot(a, b, preferred_element_type=F32)


def after(v, *others):
    return lax.optimization_barrier((v, *others))[0]


def lse(parts):
    top = parts[0]
    for p in parts[1:]:
        top = jnp.maximum(top, p)
    return top + jnp.log(sum(jnp.exp(p - top) for p in parts))


def padded(size):
    return -(-size // 128) * 128


def score_kernel(inverse, pair, *refs):
    blocks, (e, top, total) = refs[:-3], refs[-3:]
    count = sum(b.shape[0] for b in blocks)
    rest = jnp.zeros((e.shape[1] - count, pair.shape[1]), BF16)
    x = jnp.concatenate([b[...] for b in blocks] + [rest])
    s = lax.dot_general(pair[...], x, (((1,), (1,)), ((), ())), preferred_element_type=F32) * inverse
    most = jnp.max(s, axis=0, keepdims=True)
    weight = jnp.exp(s - most)
    column = lax.broadcasted_iota(jnp.int32, weight.shape, 1)
    e[...] = jnp.where(column < count, weight, 0.0).astype(BF16)
    top[...] = most
    total[...] = most + jnp.log(jnp.sum(weight, axis=0, keepdims=True))


def score(pair, blocks):
    cents, width = pair.shape
    count = padded(sum(b.shape[0] for b in blocks))
    return pl.pallas_call(
        lambda *refs: score_kernel(1.0 / (math.sqrt(width) * 0.05), *refs),
        out_shape=[
            jax.ShapeDtypeStruct((cents, count), BF16),
            jax.ShapeDtypeStruct((1, count), F32),
            jax.ShapeDtypeStruct((1, count), F32),
        ],
        compiler_params=pltpu.CompilerParams(vmem_limit_bytes=40 * 2**20),
        cost_estimate=pl.CostEstimate(
            flops=2 * cents * count * width,
            bytes_accessed=2 * (cents * width + count * width + cents * count),
            transcendentals=cents * count,
        ),
    )(pair, *blocks)


def weigh_kernel(sizes, scale, tiles, w, *refs):
    count, pieces = len(sizes), sum(len(s) for s in sizes)
    es, blocks = refs[:count], list(refs[count : count + pieces])
    near, far, counts, x, p = refs[count + pieces :]
    step = pl.program_id(0)

    @pl.when(step == 0)
    def _():
        at = 0
        for e, group in zip(es, sizes):
            stop = at + e.shape[1]
            for size in group:
                x[at : at + size] = blocks.pop(0)[...]
                at += size
            if at < stop:
                x[at:stop] = jnp.zeros((stop - at, x.shape[1]), BF16)
            at = stop

    at, masses = 0, 0.0
    for e in es:
        span = slice(at, at + e.shape[1])
        prob = e[...].astype(F32) * w[:, span]
        masses = masses + jnp.sum(prob, axis=1, keepdims=True)
        p[:, span] = prob.astype(BF16)
        at = span.stop
    counts[...] = jnp.transpose(jnp.broadcast_to(masses * scale, (masses.shape[0], 128)))[:1]
    sums = dot(p[...], x[...]) * scale

    @pl.when(step < tiles)
    def _():
        far[...] = sums.astype(BF16)

    @pl.when(step >= tiles)
    def _():
        near[...] = sums


def weigh(groups, es, w, scale):
    sizes = [[b.shape[0] for b in group] for group in groups]
    blocks = [b for group in groups for b in group]
    width = blocks[0].shape[1]
    cents = es[0].shape[0]
    passages = sum(e.shape[1] for e in es)
    tile = math.gcd(cents // 2, 256)
    tiles = cents // 2 // tile
    turn = lambda i: (i + tiles) % (2 * tiles)
    whole = lambda b: pl.BlockSpec(b.shape, lambda i: (0, 0), pipeline_mode=pl.Buffered(1))
    return pl.pallas_call(
        lambda *refs: weigh_kernel(sizes, scale, tiles, *refs),
        grid=(2 * tiles,),
        in_specs=[whole(w)]
        + [pl.BlockSpec((tile, e.shape[1]), lambda i: (turn(i), 0)) for e in es]
        + [whole(b) for b in blocks],
        out_specs=[
            pl.BlockSpec((tile, width), lambda i: (jnp.maximum(i - tiles, 0), 0)),
            pl.BlockSpec((tile, width), lambda i: (jnp.minimum(i, tiles - 1), 0)),
            pl.BlockSpec((1, tile), lambda i: (0, turn(i))),
        ],
        out_shape=[
            jax.ShapeDtypeStruct((cents // 2, width), F32),
            jax.ShapeDtypeStruct((cents // 2, width), BF16),
            jax.ShapeDtypeStruct((1, cents), F32),
        ],
        scratch_shapes=[pltpu.VMEM((passages, width), BF16), pltpu.VMEM((tile, passages), BF16)],
        compiler_params=pltpu.CompilerParams(vmem_limit_bytes=56 * 2**20),
        cost_estimate=pl.CostEstimate(
            flops=2 * cents * passages * width,
            bytes_accessed=2 * passages * (cents + width) + 8 * cents * width,
            transcendentals=0,
        ),
    )(w, *es, *blocks)


def deal_kernel(position, hidden, blocks):
    share = blocks.shape[2]
    for d in range(blocks.shape[0]):
        blocks[position[d]] = hidden[:, d * share : (d + 1) * share]


def deal(hidden, position):
    rows, hid = hidden.shape
    n = position.shape[0]
    vmem = pl.BlockSpec(memory_space=pltpu.VMEM)
    return pl.pallas_call(
        deal_kernel,
        in_specs=[pl.BlockSpec(memory_space=pltpu.SMEM), vmem],
        out_specs=vmem,
        out_shape=jax.ShapeDtypeStruct((n, rows, hid // n), hidden.dtype),
        compiler_params=pltpu.CompilerParams(vmem_limit_bytes=32 * 2**20),
        cost_estimate=pl.CostEstimate(flops=0, bytes_accessed=4 * rows * hid, transcendentals=0),
    )(position, hidden)


def arrivals(lines):
    table = []
    for z in range(lines):
        near = [(s, w, z - s if w == 0 else z + s) for s in range(1, lines) for w in (1, 0)]
        table.append([e for e in near if 0 <= e[2] < lines])
    return table


def make_body(n, lines):
    table = arrivals(lines)

    def hop(v, k):
        return lax.ppermute(v, "dp", [(i, i ^ k) for i in range(n)])

    def up(v):
        return lax.ppermute(v, "dp", [(i, i + PLANE) for i in range(n - PLANE)])

    def down(v):
        return lax.ppermute(v, "dp", [(i + PLANE, i) for i in range(n - PLANE)])

    def choose(line, values):
        out = values[-1]
        for z in range(lines - 2, -1, -1):
            if values[z] is not out:
                out = jnp.where(line <= z, values[z], out)
        return out

    def along(v):
        line = lax.axis_index("dp") // PLANE
        moved = {(0, 0): v, (0, 1): v}
        block = v
        for s in range(1, lines):
            ties = yield block
            below, above = moved[s - 1, 0], moved[s - 1, 1]
            if ties:
                below, above, *_ = lax.optimization_barrier((below, above, *ties))
            moved[s, 0], moved[s, 1] = up(below), down(above)
            block = lax.optimization_barrier(choose(line, [moved[table[z][s - 1][:2]] for z in range(lines)]))
        yield block

    def body(hidden, residual, down_weight, gain, proj_weight, centroids):
        me = lax.axis_index("dp")
        line, quad, core = me // PLANE, (me // 2) % QUAD, me % 2
        rows, hid = hidden.shape
        share = hid // n
        width = proj_weight.shape[1]
        cents = centroids.shape[0]

        orders = [[z] + [e[2] for e in table[z]] for z in range(lines)]
        place = jnp.array([[order.index(z) for z in range(lines)] for order in orders], jnp.int32)[line]
        d = jnp.arange(n)
        position = (((d // 2 % QUAD) ^ quad) * lines + place[d // PLANE]) * 2 + ((d % 2) ^ core)
        blocks = deal(hidden, position.astype(jnp.int32)).reshape(QUAD, lines, 2, rows, share)
        units = [blocks[0]] + [hop(blocks[k], 2 * k) for k in range(1, QUAD - 1)]

        down_rows = lax.all_to_all(down_weight, "dp", 0, 1, tiled=True)
        own = gain[:, None] * proj_weight.astype(F32)
        full = lax.all_gather(own, "cent", axis=0, tiled=True)
        full = full.astype(BF16)
        direct = dot(residual, own.astype(BF16))
        pair = jnp.concatenate([centroids, hop(centroids, 1)])
        last = blocks[QUAD - 1]
        down_rows, full, direct, pair, last, *units = lax.optimization_barrier(
            (down_rows, full, direct, pair, last, *units)
        )

        halves = [slice(0, width // 2), slice(width // 2, width)]
        folds = []
        for h in halves:
            source = after(down_rows, folds[0]) if folds else down_rows
            folds.append(dot(source, full[:, h]).astype(BF16))
            if not units[QUAD - 1 :]:
                last, folds[0] = lax.optimization_barrier((last, folds[0]))
                units.append(hop(last, 2 * (QUAD - 1)))
        units = jnp.concatenate(units, axis=2)
        walks = [along(f) for f in folds]
        parts = [0.0, 0.0]
        for j in range(lines):
            for i, walk in enumerate(walks):
                block = next(walk) if j == 0 else walk.send(None)
                parts[i] = parts[i] + dot(units[j, 0], block) + dot(units[j, 1], hop(block, 1))
        raws = []
        for h, part in zip(halves, parts):
            part = part.reshape(QUAD, rows, -1)
            raw = part[0] + direct[:, h]
            for k in range(1, QUAD):
                raw = raw + hop(part[k].astype(BF16), 2 * k).astype(F32)
            raws.append(raw)
        raw = jnp.concatenate(raws, axis=1)
        raw = lax.psum(raw, "cent")
        embed = (raw * lax.rsqrt(jnp.mean(raw * raw, axis=1, keepdims=True) + 1e-06)).astype(BF16)

        def spread(block):
            return [block, hop(block, 2), hop(block, 4)]

        scale_up = cents * n * lax.axis_size("cent") / (rows * n)
        groups, tags, scored = [], [], []

        def take(blocks, names):
            groups.append(blocks)
            tags.append(names)
            scored.append(score(pair, blocks))

        first = spread(embed)
        lined = [None] + [hop(embed if k < 3 else after(embed, first[1]), k * PLANE) for k in range(1, lines)]
        take(first + [hop(first[1], 4)], [(0, q) for q in (0, 1, 2, 3)])
        late, late_names, ends, end_names = [], [], [], []
        for k in range(1, lines):
            wait = scored[k // 2 - 1][2] if k % 2 == 0 else scored[0][2] if k > 1 else None
            got = spread(lined[k] if wait is None else after(lined[k], wait))
            names = [(k, 0), (k, 1), (k, 2)]
            end = (2, 1) if k % 2 == 1 else (1, 2)
            start = got[end[0]]
            if k == 1:
                take(got + [hop(start, 2 * end[1])], names + [(k, 3)])
            else:
                late, late_names = late + got, late_names + names
                ends.append(hop(after(start, scored[1][2]), 2 * end[1]))
                end_names.append((k, 3))
        take(late, late_names)
        ends = lax.optimization_barrier((*ends, scored[-1][2]))[:-1]
        take(list(ends), end_names)

        parts = {}
        for names, (_, _, total) in zip(tags, scored):
            for i, name in enumerate(names):
                parts[name] = total[:, i * rows : (i + 1) * rows]
        v = jnp.stack([jnp.concatenate([parts[k, q] for q in range(QUAD)]) for k in range(lines)])
        got = [v] + [hop(v, 2 * k) for k in range(1, QUAD)]
        v = lse([jnp.stack([g[:, j ^ k] for j in range(QUAD)], axis=1) for k, g in enumerate(got)])
        got = [v] + [hop(v, PLANE * k) for k in range(1, lines)]
        v = lse([jnp.stack([g[j ^ k] for j in range(lines)]) for k, g in enumerate(got)])
        if lax.axis_size("cent") > 1:
            top = lax.pmax(v, "cent")
            v = top + jnp.log(lax.psum(jnp.exp(v - top), "cent"))
        tops = jnp.concatenate([top for _, top, _ in scored], axis=1)
        logs = []
        for names, (_, top, _) in zip(tags, scored):
            logs += [v[k, q] for k, q in names]
            logs.append(jnp.zeros(top.shape[1] - len(names) * rows, F32))
        w = jnp.exp(tops - jnp.concatenate(logs)[None])

        near, far, masses = weigh(groups, [e for e, _, _ in scored], w, scale_up)
        weighted = near + hop(far, 1).astype(F32)
        counts = masses[0, :cents] + hop(masses[0, cents:], 1)
        return weighted, counts

    return body


def solution(mesh):
    n = mesh.shape["dp"]
    in_specs = (
        P("dp", "cent"),
        P("dp", "cent"),
        P("cent", "dp"),
        P("cent"),
        P("cent", None),
        P(("dp", "cent"), None),
    )
    out_specs = (P(("dp", "cent"), None), P(("dp", "cent")))
    return jax.shard_map(
        make_body(n, n // PLANE), mesh=mesh, in_specs=in_specs, out_specs=out_specs, check_vma=False
    )
```

```python
import math

import jax
import jax.numpy as jnp
from jax import lax
from jax.experimental import pallas as pl
from jax.experimental.pallas import tpu as pltpu
from jax.sharding import PartitionSpec as P


F32 = jnp.float32
BF16 = jnp.bfloat16
PLANE = 8
QUAD = 4


def dot(a, b):
    return jnp.dot(a, b, preferred_element_type=F32)


def after(v, *others):
    return lax.optimization_barrier((v, *others))[0]


def lse(parts):
    top = parts[0]
    for p in parts[1:]:
        top = jnp.maximum(top, p)
    return top + jnp.log(sum(jnp.exp(p - top) for p in parts))


def padded(size):
    return -(-size // 128) * 128


def score_kernel(inverse, pair, *refs):
    blocks, (e, top, total) = refs[:-3], refs[-3:]
    count = sum(b.shape[0] for b in blocks)
    rest = jnp.zeros((e.shape[1] - count, pair.shape[1]), BF16)
    x = jnp.concatenate([b[...] for b in blocks] + [rest])
    s = lax.dot_general(pair[...], x, (((1,), (1,)), ((), ())), preferred_element_type=F32) * inverse
    most = jnp.max(s, axis=0, keepdims=True)
    weight = jnp.exp(s - most)
    column = lax.broadcasted_iota(jnp.int32, weight.shape, 1)
    e[...] = jnp.where(column < count, weight, 0.0).astype(BF16)
    top[...] = most
    total[...] = most + jnp.log(jnp.sum(weight, axis=0, keepdims=True))


def score(pair, blocks):
    cents, width = pair.shape
    count = padded(sum(b.shape[0] for b in blocks))
    return pl.pallas_call(
        lambda *refs: score_kernel(1.0 / (math.sqrt(width) * 0.05), *refs),
        out_shape=[
            jax.ShapeDtypeStruct((cents, count), BF16),
            jax.ShapeDtypeStruct((1, count), F32),
            jax.ShapeDtypeStruct((1, count), F32),
        ],
        compiler_params=pltpu.CompilerParams(vmem_limit_bytes=40 * 2**20),
        cost_estimate=pl.CostEstimate(
            flops=2 * cents * count * width,
            bytes_accessed=2 * (cents * width + count * width + cents * count),
            transcendentals=cents * count,
        ),
    )(pair, *blocks)


def weigh_kernel(sizes, scale, tiles, w, *refs):
    count, pieces = len(sizes), sum(len(s) for s in sizes)
    es, blocks = refs[:count], list(refs[count : count + pieces])
    near, far, counts, x, p = refs[count + pieces :]
    step = pl.program_id(0)

    @pl.when(step == 0)
    def _():
        at = 0
        for e, group in zip(es, sizes):
            stop = at + e.shape[1]
            for size in group:
                x[at : at + size] = blocks.pop(0)[...]
                at += size
            if at < stop:
                x[at:stop] = jnp.zeros((stop - at, x.shape[1]), BF16)
            at = stop

    at, masses = 0, 0.0
    for e in es:
        span = slice(at, at + e.shape[1])
        prob = e[...].astype(F32) * w[:, span]
        masses = masses + jnp.sum(prob, axis=1, keepdims=True)
        p[:, span] = prob.astype(BF16)
        at = span.stop
    counts[...] = jnp.transpose(jnp.broadcast_to(masses * scale, (masses.shape[0], 128)))[:1]
    sums = dot(p[...], x[...]) * scale

    @pl.when(step < tiles)
    def _():
        far[...] = sums.astype(BF16)

    @pl.when(step >= tiles)
    def _():
        near[...] = sums.astype(BF16)


def weigh(groups, es, w, scale):
    sizes = [[b.shape[0] for b in group] for group in groups]
    blocks = [b for group in groups for b in group]
    width = blocks[0].shape[1]
    cents = es[0].shape[0]
    passages = sum(e.shape[1] for e in es)
    tile = math.gcd(cents // 2, 256)
    tiles = cents // 2 // tile
    turn = lambda i: (i + tiles) % (2 * tiles)
    whole = lambda b: pl.BlockSpec(b.shape, lambda i: (0, 0), pipeline_mode=pl.Buffered(1))
    return pl.pallas_call(
        lambda *refs: weigh_kernel(sizes, scale, tiles, *refs),
        grid=(2 * tiles,),
        in_specs=[whole(w)]
        + [pl.BlockSpec((tile, e.shape[1]), lambda i: (turn(i), 0)) for e in es]
        + [whole(b) for b in blocks],
        out_specs=[
            pl.BlockSpec((tile, width), lambda i: (jnp.maximum(i - tiles, 0), 0)),
            pl.BlockSpec((tile, width), lambda i: (jnp.minimum(i, tiles - 1), 0)),
            pl.BlockSpec((1, tile), lambda i: (0, turn(i))),
        ],
        out_shape=[
            jax.ShapeDtypeStruct((cents // 2, width), BF16),
            jax.ShapeDtypeStruct((cents // 2, width), BF16),
            jax.ShapeDtypeStruct((1, cents), F32),
        ],
        scratch_shapes=[pltpu.VMEM((passages, width), BF16), pltpu.VMEM((tile, passages), BF16)],
        compiler_params=pltpu.CompilerParams(vmem_limit_bytes=56 * 2**20),
        cost_estimate=pl.CostEstimate(
            flops=2 * cents * passages * width,
            bytes_accessed=2 * passages * (cents + width) + 8 * cents * width,
            transcendentals=0,
        ),
    )(w, *es, *blocks)


def deal_kernel(position, hidden, blocks):
    share = blocks.shape[2]
    for d in range(blocks.shape[0]):
        blocks[position[d]] = hidden[:, d * share : (d + 1) * share]


def deal(hidden, position):
    rows, hid = hidden.shape
    n = position.shape[0]
    vmem = pl.BlockSpec(memory_space=pltpu.VMEM)
    return pl.pallas_call(
        deal_kernel,
        in_specs=[pl.BlockSpec(memory_space=pltpu.SMEM), vmem],
        out_specs=vmem,
        out_shape=jax.ShapeDtypeStruct((n, rows, hid // n), hidden.dtype),
        compiler_params=pltpu.CompilerParams(vmem_limit_bytes=32 * 2**20),
        cost_estimate=pl.CostEstimate(flops=0, bytes_accessed=4 * rows * hid, transcendentals=0),
    )(position, hidden)


def arrivals(lines):
    table = []
    for z in range(lines):
        near = [(s, w, z - s if w == 0 else z + s) for s in range(1, lines) for w in (1, 0)]
        table.append([e for e in near if 0 <= e[2] < lines])
    return table


def make_body(n, lines):
    table = arrivals(lines)

    def hop(v, k):
        return lax.ppermute(v, "dp", [(i, i ^ k) for i in range(n)])

    def up(v):
        return lax.ppermute(v, "dp", [(i, i + PLANE) for i in range(n - PLANE)])

    def down(v):
        return lax.ppermute(v, "dp", [(i + PLANE, i) for i in range(n - PLANE)])

    def choose(line, values):
        out = values[-1]
        for z in range(lines - 2, -1, -1):
            if values[z] is not out:
                out = jnp.where(line <= z, values[z], out)
        return out

    def along(v):
        line = lax.axis_index("dp") // PLANE
        moved = {(0, 0): v, (0, 1): v}
        block = v
        for s in range(1, lines):
            ties = yield block
            below, above = moved[s - 1, 0], moved[s - 1, 1]
            if ties:
                below, above, *_ = lax.optimization_barrier((below, above, *ties))
            moved[s, 0], moved[s, 1] = up(below), down(above)
            block = lax.optimization_barrier(choose(line, [moved[table[z][s - 1][:2]] for z in range(lines)]))
        yield block

    def body(hidden, residual, down_weight, gain, proj_weight, centroids):
        me = lax.axis_index("dp")
        line, quad, core = me // PLANE, (me // 2) % QUAD, me % 2
        rows, hid = hidden.shape
        share = hid // n
        width = proj_weight.shape[1]
        cents = centroids.shape[0]

        orders = [[z] + [e[2] for e in table[z]] for z in range(lines)]
        place = jnp.array([[order.index(z) for z in range(lines)] for order in orders], jnp.int32)[line]
        d = jnp.arange(n)
        position = (((d // 2 % QUAD) ^ quad) * lines + place[d // PLANE]) * 2 + ((d % 2) ^ core)
        blocks = deal(hidden, position.astype(jnp.int32)).reshape(QUAD, lines, 2, rows, share)
        units = [blocks[0]] + [hop(blocks[k], 2 * k) for k in range(1, QUAD - 1)]

        down_rows = lax.all_to_all(down_weight, "dp", 0, 1, tiled=True)
        own = gain[:, None] * proj_weight.astype(F32)
        full = lax.all_gather(own, "cent", axis=0, tiled=True)
        full = full.astype(BF16)
        direct = dot(residual, own.astype(BF16))
        pair = jnp.concatenate([centroids, hop(centroids, 1)])
        last = blocks[QUAD - 1]
        halves = [slice(0, width // 2), slice(width // 2, width)]
        down_rows, heads, direct, pair, last, units = lax.optimization_barrier(
            (down_rows, [full[:, h] for h in halves], direct, pair, last, units)
        )

        folds = []
        for head in heads:
            source = after(down_rows, folds[0]) if folds else down_rows
            folds.append(dot(source, head).astype(BF16))
            if not units[QUAD - 1 :]:
                last, folds[0] = lax.optimization_barrier((last, folds[0]))
                units.append(hop(last, 2 * (QUAD - 1)))
        units = jnp.concatenate(units, axis=2)
        walks = [along(f) for f in folds]
        parts = [0.0, 0.0]
        for j in range(lines):
            for i, walk in enumerate(walks):
                block = next(walk) if j == 0 else walk.send(None)
                parts[i] = parts[i] + dot(units[j, 0], block) + dot(units[j, 1], hop(block, 1))
        raws = []
        for h, part in zip(halves, parts):
            part = part.reshape(QUAD, rows, -1)
            raw = part[0] + direct[:, h]
            for k in range(1, QUAD):
                raw = raw + hop(part[k].astype(BF16), 2 * k).astype(F32)
            raws.append(raw)
        raw = jnp.concatenate(raws, axis=1)
        raw = lax.psum(raw, "cent")
        embed = (raw * lax.rsqrt(jnp.mean(raw * raw, axis=1, keepdims=True) + 1e-06)).astype(BF16)

        def spread(block):
            return [block, hop(block, 2), hop(block, 4)]

        scale_up = cents * n * lax.axis_size("cent") / (rows * n)
        groups, tags, scored = [], [], []

        def take(blocks, names):
            groups.append(blocks)
            tags.append(names)
            scored.append(score(pair, blocks))

        first = spread(embed)
        lined = [None] + [hop(embed if k < 3 else after(embed, first[1]), k * PLANE) for k in range(1, lines)]
        take(first + [hop(first[1], 4)], [(0, q) for q in (0, 1, 2, 3)])
        late, late_names, ends, end_names = [], [], [], []
        for k in range(1, lines):
            wait = scored[k // 2 - 1][2] if k % 2 == 0 else scored[0][2] if k > 1 else None
            got = spread(lined[k] if wait is None else after(lined[k], wait))
            names = [(k, 0), (k, 1), (k, 2)]
            end = (2, 1) if k % 2 == 1 else (1, 2)
            start = got[end[0]]
            if k == 1:
                take(got + [hop(start, 2 * end[1])], names + [(k, 3)])
            else:
                late, late_names = late + got, late_names + names
                ends.append(hop(after(start, scored[1][2]), 2 * end[1]))
                end_names.append((k, 3))
        take(late, late_names)
        ends = lax.optimization_barrier((*ends, scored[-1][2]))[:-1]
        take(list(ends), end_names)

        parts = {}
        for names, (_, _, total) in zip(tags, scored):
            for i, name in enumerate(names):
                parts[name] = total[:, i * rows : (i + 1) * rows]
        v = jnp.stack([jnp.concatenate([parts[k, q] for q in range(QUAD)]) for k in range(lines)])
        got = [v] + [hop(v, 2 * k) for k in range(1, QUAD)]
        v = lse([jnp.stack([g[:, j ^ k] for j in range(QUAD)], axis=1) for k, g in enumerate(got)])
        got = [v] + [hop(v, PLANE * k) for k in range(1, lines)]
        v = lse([jnp.stack([g[j ^ k] for j in range(lines)]) for k, g in enumerate(got)])
        if lax.axis_size("cent") > 1:
            top = lax.pmax(v, "cent")
            v = top + jnp.log(lax.psum(jnp.exp(v - top), "cent"))
        tops = jnp.concatenate([top for _, top, _ in scored], axis=1)
        logs = []
        for names, (_, top, _) in zip(tags, scored):
            logs += [v[k, q] for k, q in names]
            logs.append(jnp.zeros(top.shape[1] - len(names) * rows, F32))
        w = jnp.exp(tops - jnp.concatenate(logs)[None])

        near, far, masses = weigh(groups, [e for e, _, _ in scored], w, scale_up)
        weighted = near.astype(F32) + hop(far, 1).astype(F32)
        counts = masses[0, :cents] + hop(masses[0, cents:], 1)
        return weighted, counts

    return body


def solution(mesh):
    n = mesh.shape["dp"]
    in_specs = (
        P("dp", "cent"),
        P("dp", "cent"),
        P("cent", "dp"),
        P("cent"),
        P("cent", None),
        P(("dp", "cent"), None),
    )
    out_specs = (P(("dp", "cent"), None), P(("dp", "cent")))
    return jax.shard_map(
        make_body(n, n // PLANE), mesh=mesh, in_specs=in_specs, out_specs=out_specs, check_vma=False
    )
```

```python
import math

import jax
import jax.numpy as jnp
from jax import lax
from jax.experimental import pallas as pl
from jax.experimental.pallas import tpu as pltpu
from jax.sharding import PartitionSpec as P


F32 = jnp.float32
BF16 = jnp.bfloat16
PLANE = 8
QUAD = 4


def dot(a, b):
    return jnp.dot(a, b, preferred_element_type=F32)


def after(v, *others):
    return lax.optimization_barrier((v, *others))[0]


def lse(parts):
    top = parts[0]
    for p in parts[1:]:
        top = jnp.maximum(top, p)
    return top + jnp.log(sum(jnp.exp(p - top) for p in parts))


def padded(size):
    return -(-size // 128) * 128


def score_kernel(inverse, pair, *refs):
    blocks, (e, top, total) = refs[:-3], refs[-3:]
    count = sum(b.shape[0] for b in blocks)
    rest = jnp.zeros((e.shape[1] - count, pair.shape[1]), BF16)
    x = jnp.concatenate([b[...] for b in blocks] + [rest])
    s = lax.dot_general(pair[...], x, (((1,), (1,)), ((), ())), preferred_element_type=F32) * inverse
    most = jnp.max(s, axis=0, keepdims=True)
    weight = jnp.exp(s - most)
    column = lax.broadcasted_iota(jnp.int32, weight.shape, 1)
    e[...] = jnp.where(column < count, weight, 0.0).astype(BF16)
    top[...] = most
    total[...] = most + jnp.log(jnp.sum(weight, axis=0, keepdims=True))


def score(pair, blocks):
    cents, width = pair.shape
    count = padded(sum(b.shape[0] for b in blocks))
    return pl.pallas_call(
        lambda *refs: score_kernel(1.0 / (math.sqrt(width) * 0.05), *refs),
        out_shape=[
            jax.ShapeDtypeStruct((cents, count), BF16),
            jax.ShapeDtypeStruct((1, count), F32),
            jax.ShapeDtypeStruct((1, count), F32),
        ],
        compiler_params=pltpu.CompilerParams(vmem_limit_bytes=40 * 2**20),
        cost_estimate=pl.CostEstimate(
            flops=2 * cents * count * width,
            bytes_accessed=2 * (cents * width + count * width + cents * count),
            transcendentals=cents * count,
        ),
    )(pair, *blocks)


def weigh_kernel(sizes, scale, tiles, w, *refs):
    count, pieces = len(sizes), sum(len(s) for s in sizes)
    es, blocks = refs[:count], list(refs[count : count + pieces])
    near, far, counts, x, p = refs[count + pieces :]
    step = pl.program_id(0)

    @pl.when(step == 0)
    def _():
        at = 0
        for e, group in zip(es, sizes):
            stop = at + e.shape[1]
            for size in group:
                x[at : at + size] = blocks.pop(0)[...]
                at += size
            if at < stop:
                x[at:stop] = jnp.zeros((stop - at, x.shape[1]), BF16)
            at = stop

    at, masses = 0, 0.0
    for e in es:
        span = slice(at, at + e.shape[1])
        prob = e[...].astype(F32) * w[:, span]
        masses = masses + jnp.sum(prob, axis=1, keepdims=True)
        p[:, span] = prob.astype(BF16)
        at = span.stop
    counts[...] = jnp.transpose(jnp.broadcast_to(masses * scale, (masses.shape[0], 128)))[:1]
    sums = dot(p[...], x[...]) * scale

    @pl.when(step < tiles)
    def _():
        far[...] = sums.astype(BF16)

    @pl.when(step >= tiles)
    def _():
        near[...] = sums.astype(BF16)


def weigh(groups, es, w, scale):
    sizes = [[b.shape[0] for b in group] for group in groups]
    blocks = [b for group in groups for b in group]
    width = blocks[0].shape[1]
    cents = es[0].shape[0]
    passages = sum(e.shape[1] for e in es)
    tile = math.gcd(cents // 2, 256)
    tiles = cents // 2 // tile
    turn = lambda i: (i + tiles) % (2 * tiles)
    whole = lambda b: pl.BlockSpec(b.shape, lambda i: (0, 0), pipeline_mode=pl.Buffered(1))
    return pl.pallas_call(
        lambda *refs: weigh_kernel(sizes, scale, tiles, *refs),
        grid=(2 * tiles,),
        in_specs=[whole(w)]
        + [pl.BlockSpec((tile, e.shape[1]), lambda i: (turn(i), 0)) for e in es]
        + [whole(b) for b in blocks],
        out_specs=[
            pl.BlockSpec((tile, width), lambda i: (jnp.maximum(i - tiles, 0), 0)),
            pl.BlockSpec((tile, width), lambda i: (jnp.minimum(i, tiles - 1), 0)),
            pl.BlockSpec((1, tile), lambda i: (0, turn(i))),
        ],
        out_shape=[
            jax.ShapeDtypeStruct((cents // 2, width), BF16),
            jax.ShapeDtypeStruct((cents // 2, width), BF16),
            jax.ShapeDtypeStruct((1, cents), F32),
        ],
        scratch_shapes=[pltpu.VMEM((passages, width), BF16), pltpu.VMEM((tile, passages), BF16)],
        compiler_params=pltpu.CompilerParams(vmem_limit_bytes=56 * 2**20),
        cost_estimate=pl.CostEstimate(
            flops=2 * cents * passages * width,
            bytes_accessed=2 * passages * (cents + width) + 8 * cents * width,
            transcendentals=0,
        ),
    )(w, *es, *blocks)


def deal_kernel(position, hidden, blocks):
    share = blocks.shape[2]
    for d in range(blocks.shape[0]):
        blocks[position[d]] = hidden[:, d * share : (d + 1) * share]


def deal(hidden, position):
    rows, hid = hidden.shape
    n = position.shape[0]
    vmem = pl.BlockSpec(memory_space=pltpu.VMEM)
    return pl.pallas_call(
        deal_kernel,
        in_specs=[pl.BlockSpec(memory_space=pltpu.SMEM), vmem],
        out_specs=vmem,
        out_shape=jax.ShapeDtypeStruct((n, rows, hid // n), hidden.dtype),
        compiler_params=pltpu.CompilerParams(vmem_limit_bytes=32 * 2**20),
        cost_estimate=pl.CostEstimate(flops=0, bytes_accessed=4 * rows * hid, transcendentals=0),
    )(position, hidden)


def arrivals(lines):
    table = []
    for z in range(lines):
        near = [(s, w, z - s if w == 0 else z + s) for s in range(1, lines) for w in (1, 0)]
        table.append([e for e in near if 0 <= e[2] < lines])
    return table


def make_body(n, lines):
    table = arrivals(lines)

    def hop(v, k):
        return lax.ppermute(v, "dp", [(i, i ^ k) for i in range(n)])

    def up(v):
        return lax.ppermute(v, "dp", [(i, i + PLANE) for i in range(n - PLANE)])

    def down(v):
        return lax.ppermute(v, "dp", [(i + PLANE, i) for i in range(n - PLANE)])

    def choose(line, values):
        out = values[-1]
        for z in range(lines - 2, -1, -1):
            if values[z] is not out:
                out = jnp.where(line <= z, values[z], out)
        return out

    def along(v):
        line = lax.axis_index("dp") // PLANE
        moved = {(0, 0): v, (0, 1): v}
        block = v
        for s in range(1, lines):
            ties = yield block
            below, above = moved[s - 1, 0], moved[s - 1, 1]
            if ties:
                below, above, *_ = lax.optimization_barrier((below, above, *ties))
            moved[s, 0], moved[s, 1] = up(below), down(above)
            block = lax.optimization_barrier(choose(line, [moved[table[z][s - 1][:2]] for z in range(lines)]))
        yield block

    def body(hidden, residual, down_weight, gain, proj_weight, centroids):
        me = lax.axis_index("dp")
        line, quad, core = me // PLANE, (me // 2) % QUAD, me % 2
        rows, hid = hidden.shape
        share = hid // n
        width = proj_weight.shape[1]
        cents = centroids.shape[0]

        orders = [[z] + [e[2] for e in table[z]] for z in range(lines)]
        place = jnp.array([[order.index(z) for z in range(lines)] for order in orders], jnp.int32)[line]
        d = jnp.arange(n)
        position = (((d // 2 % QUAD) ^ quad) * lines + place[d // PLANE]) * 2 + ((d % 2) ^ core)
        blocks = deal(hidden, position.astype(jnp.int32)).reshape(QUAD, lines, 2, rows, share)
        units = [blocks[0]] + [hop(blocks[k], 2 * k) for k in range(1, QUAD - 1)]

        down_rows = lax.all_to_all(down_weight, "dp", 0, 1, tiled=True)
        own = gain[:, None] * proj_weight.astype(F32)
        full = lax.all_gather(own, "cent", axis=0, tiled=True)
        full = full.astype(BF16)
        direct = dot(residual, own.astype(BF16))
        pair = jnp.concatenate([centroids, hop(centroids, 1)])
        last = blocks[QUAD - 1]
        halves = [slice(0, width // 2), slice(width // 2, width)]
        down_rows, heads, direct, pair, last, units = lax.optimization_barrier(
            (down_rows, [full[:, h] for h in halves], direct, pair, last, units)
        )

        folds = []
        for head in heads:
            source = after(down_rows, folds[0]) if folds else down_rows
            folds.append(dot(source, head).astype(BF16))
            if not units[QUAD - 1 :]:
                last, folds[0] = lax.optimization_barrier((last, folds[0]))
                units.append(hop(last, 2 * (QUAD - 1)))
        units = jnp.concatenate(units, axis=2)
        walks = [along(f) for f in folds]
        parts = [0.0, 0.0]
        for j in range(lines):
            for i, walk in enumerate(walks):
                block = next(walk) if j == 0 else walk.send(None)
                parts[i] = parts[i] + dot(units[j, 0], block) + dot(units[j, 1], hop(block, 1))
        raws = []
        for h, part in zip(halves, parts):
            part = part.reshape(QUAD, rows, -1)
            raw = part[0] + direct[:, h]
            for k in range(1, QUAD):
                raw = raw + hop(part[k].astype(BF16), 2 * k).astype(F32)
            raws.append(raw)
        raw = jnp.concatenate(raws, axis=1)
        raw = lax.psum(raw, "cent")
        embed = (raw * lax.rsqrt(jnp.mean(raw * raw, axis=1, keepdims=True) + 1e-06)).astype(BF16)

        def spread(block):
            return [block, hop(block, 2), hop(block, 4)]

        scale_up = cents * n * lax.axis_size("cent") / (rows * n)
        groups, tags, scored = [], [], []

        def take(blocks, names):
            groups.append(blocks)
            tags.append(names)
            scored.append(score(pair, blocks))

        first = spread(embed)
        lined = [None] + [hop(embed, k * PLANE) for k in range(1, lines)]
        take(first + [hop(first[1], 4)], [(0, q) for q in (0, 1, 2, 3)])
        late, late_names, ends, end_names = [], [], [], []
        for k in range(1, lines):
            wait = scored[k // 2 - 1][2] if k % 2 == 0 else scored[0][2] if k > 1 else None
            got = spread(lined[k] if wait is None else after(lined[k], wait))
            names = [(k, 0), (k, 1), (k, 2)]
            end = (2, 1) if k % 2 == 1 else (1, 2)
            start = got[end[0]]
            if k == 1:
                take(got + [hop(start, 2 * end[1])], names + [(k, 3)])
            else:
                late, late_names = late + got, late_names + names
                ends.append(hop(after(start, scored[1][2]), 2 * end[1]))
                end_names.append((k, 3))
        take(late, late_names)
        ends = lax.optimization_barrier((*ends, scored[-1][2]))[:-1]
        take(list(ends), end_names)

        parts = {}
        for names, (_, _, total) in zip(tags, scored):
            for i, name in enumerate(names):
                parts[name] = total[:, i * rows : (i + 1) * rows]
        v = jnp.stack([jnp.concatenate([parts[k, q] for q in range(QUAD)]) for k in range(lines)])
        got = [v] + [hop(v, 2 * k) for k in range(1, QUAD)]
        v = lse([jnp.stack([g[:, j ^ k] for j in range(QUAD)], axis=1) for k, g in enumerate(got)])
        got = [v] + [hop(v, PLANE * k) for k in range(1, lines)]
        v = lse([jnp.stack([g[j ^ k] for j in range(lines)]) for k, g in enumerate(got)])
        if lax.axis_size("cent") > 1:
            top = lax.pmax(v, "cent")
            v = top + jnp.log(lax.psum(jnp.exp(v - top), "cent"))
        tops = jnp.concatenate([top for _, top, _ in scored], axis=1)
        logs = []
        for names, (_, top, _) in zip(tags, scored):
            logs += [v[k, q] for k, q in names]
            logs.append(jnp.zeros(top.shape[1] - len(names) * rows, F32))
        w = jnp.exp(tops - jnp.concatenate(logs)[None])

        near, far, masses = weigh(groups, [e for e, _, _ in scored], w, scale_up)
        weighted = near.astype(F32) + hop(far, 1).astype(F32)
        counts = masses[0, :cents] + hop(masses[0, cents:], 1)
        return weighted, counts

    return body


def solution(mesh):
    n = mesh.shape["dp"]
    in_specs = (
        P("dp", "cent"),
        P("dp", "cent"),
        P("cent", "dp"),
        P("cent"),
        P("cent", None),
        P(("dp", "cent"), None),
    )
    out_specs = (P(("dp", "cent"), None), P(("dp", "cent")))
    return jax.shard_map(
        make_body(n, n // PLANE), mesh=mesh, in_specs=in_specs, out_specs=out_specs, check_vma=False
    )
```
